256 devices in a mesh: dp: 32 (over y, z_lo, core), tensor: 8 (over x, z_hi).
Axes of the slice: x: 4, y: 4, z: 8 (z_hi: 2, z_lo: 4; z = z_hi * 4 + z_lo), core: 2. Of those that a mesh axis runs over, the one named last changes fastest.
Arguments:
- attention_output: bfloat16 [32768, 8192], P('dp', 'tensor'), may hold values from -6 to 6
- output_gradient: bfloat16 [32768, 4096], P(('dp', 'tensor')), may hold values from -24 to 24
- codes: bfloat16 [8192, 4096], P('tensor', 'dp'), may hold values from -4 to 4
- block_scale_values: float32 [64, 32], P('tensor', 'dp'), may hold values from 0.004 to 0.02
- adapter_down_factor: bfloat16 [8192, 64], P('tensor'), may hold values from -0.0625 to 0.0625
- adapter_up_factor: bfloat16 [64, 4096], replicated, may hold values from -0.0625 to 0.0625
Outputs:
- input_gradient: bfloat16 [32768, 8192], P('dp', 'tensor')
- down_factor_gradient: float32 [8192, 64], P('tensor')
- up_factor_gradient: float32 [64, 4096], P(None, 'dp')
The draws below stay inside these ranges and needn't reach their ends.
All inputs are finite; a program needn't handle non-finite values.
Results may differ from the reference program's by a relative error of at most 0.0049.
Values may be sent and summed in bfloat16 or wider, within the bound.
No kernel may reach another device: no remote copies, remote signals or barrier semaphores. Data moves between devices by JAX's collectives and lax.ppermute only.
A program may use at most 128 MiB of HBM per device.

```python
import math
import jax
import jax.numpy as jnp
from jax import lax

MODEL_WIDTH = 8192
OUTPUT_FEATURES = 4096
ADAPTER_RANK = 64
BLOCK = 128
TOKENS = 32768


def strengthened(array, own_key, source, target, blocks, factor):
    def block_of(dim):
        return (jnp.arange(array.shape[dim]) // (array.shape[dim] // blocks)).reshape((-1,) + (1,) * (array.ndim - 1 - dim))

    one_side = jax.random.permutation(own_key, blocks)[block_of(target)]
    other_side = (block_of(target) + blocks // 2) % blocks
    return jnp.where((block_of(source) == one_side) | (block_of(source) == other_side), factor * array, array)


def shard_levels(stream_key, extent, pieces, low, largest):
    factor_of, own = 1.0, jax.random.fold_in(stream_key, 6)
    for axis_at, shards_of in pieces:
        draws = jnp.exp(jax.random.uniform(jax.random.fold_in(own, axis_at), (shards_of,), jnp.float32, low / len(pieces), largest / len(pieces)))
        factor_of = factor_of * jnp.repeat(draws, extent[axis_at] // shards_of).reshape([-1 if axis == axis_at else 1 for axis in range(len(extent))])
    return factor_of


def noise(key, dims, scale, limit, pieces=(), dtype=jnp.bfloat16):
    loudness = shard_levels(key, dims, pieces, -0.22, 0.18) if pieces else 1.0
    drawn = jax.random.normal(key, dims, jnp.float32) * scale * loudness
    return jnp.minimum(jnp.maximum(drawn, -limit), limit).astype(dtype)


def heavy_noise(own_key, dims, deviation, bound, shards, heavy, kind=jnp.bfloat16):
    entries = deviation * jax.random.normal(own_key, dims, jnp.float32)
    if shards:
        entries = entries * shard_levels(own_key, dims, shards, -0.22, 0.18)
    return jnp.clip(strengthened(entries, jax.random.fold_in(own_key, 3), *heavy), -bound, bound).astype(kind)


def setup_inputs(seed: int = 0) -> dict:
    keys = jax.random.split(jax.random.key(seed), 7)
    return {
        "attention_output": noise(keys[0], (TOKENS, MODEL_WIDTH), 1.0, 6.0, ((0, 32), (1, 8))),
        "output_gradient": heavy_noise(keys[1], (TOKENS, OUTPUT_FEATURES), 1.0, 24.0, ((0, 256),), (0, 1, 256, 6.0)),
        "codes": noise(keys[2], (MODEL_WIDTH, OUTPUT_FEATURES), 1.0, 4.0, ((0, 8), (1, 32))),
        "block_scale_values": jnp.clip(jnp.exp(math.log(0.02) - 1.6094378 * jax.random.uniform(keys[3], (MODEL_WIDTH // BLOCK, OUTPUT_FEATURES // BLOCK), jnp.float32) ** shard_levels(keys[3], (MODEL_WIDTH // BLOCK, OUTPUT_FEATURES // BLOCK), ((0, 8), (1, 32)), -0.2, 0.2)), 0.004, 0.02),
        "adapter_down_factor": noise(keys[4], (MODEL_WIDTH, ADAPTER_RANK), MODEL_WIDTH ** -0.5, 0.0625, ((0, 8),)),
        "adapter_up_factor": noise(keys[5], (ADAPTER_RANK, OUTPUT_FEATURES), MODEL_WIDTH ** -0.5, 0.0625),
    }


adapter_scale = 2.0
loss_scale_factor = 64.0


def reference(attention_output, output_gradient, codes, block_scale_values, adapter_down_factor, adapter_up_factor):
    expanded = jnp.repeat(jnp.repeat(block_scale_values, BLOCK, axis=0), BLOCK, axis=1)
    weights = (codes.astype(jnp.float32) * expanded).astype(jnp.bfloat16)
    adapter_output = jnp.dot(attention_output, adapter_down_factor, preferred_element_type=jnp.float32).astype(jnp.bfloat16)
    projected_rows = lax.dot_general(output_gradient, adapter_up_factor, (((1,), (1,)), ((), ())), preferred_element_type=jnp.float32).astype(jnp.bfloat16)
    base_gradient_part = lax.dot_general(output_gradient, weights, (((1,), (1,)), ((), ())), preferred_element_type=jnp.float32)
    adapter_gradient_part = lax.dot_general(projected_rows, adapter_down_factor, (((1,), (1,)), ((), ())), preferred_element_type=jnp.float32)
    input_gradient = (base_gradient_part + adapter_scale * adapter_gradient_part).astype(jnp.bfloat16)
    scale_factor = adapter_scale / loss_scale_factor
    down_factor_gradient = scale_factor * jnp.dot(attention_output.T, projected_rows, preferred_element_type=jnp.float32)
    up_factor_gradient = scale_factor * jnp.dot(adapter_output.T, output_gradient, preferred_element_type=jnp.float32)
    return input_gradient, down_factor_gradient, up_factor_gradient
```

```python
import functools

import jax
import jax.numpy as jnp
from jax import lax
from jax.experimental import pallas as pl
from jax.experimental.pallas import tpu as pltpu
from jax.sharding import PartitionSpec as P

BLOCK = 128
NX = 4
ROWS = 128
K_CHUNK = 1024
M_TILE = 256

adapter_scale = 2.0
loss_scale_factor = 64.0


def hi_swap(value):
    return lax.ppermute(value, "tensor", [(t, t ^ 1) for t in range(2 * NX)])


def x_shift(value, step):
    return lax.ppermute(
        value,
        "tensor",
        [(t, ((t // 2 + step) % NX) * 2 + t % 2) for t in range(2 * NX)],
    )


def x_gather(own):
    half = own.shape[0] // 2
    before = x_shift(own, 1)
    after = x_shift(own, -1)
    far_top = x_shift(before[:half], 1)
    far_bottom = x_shift(after[half:], -1)
    return [(own, 0, 0), (before, -1, 0), (after, 1, 0), (far_top, 2, 0), (far_bottom, 2, half)]


def product_kernel(places, count, *refs):
    pieces = refs[:count]
    weights, projected, down, out, g_all, w_all, total, g_sem, w_sem = refs[count:]
    tensor = lax.axis_index("tensor")
    x, hi = tensor // 2, tensor % 2
    chunks = w_all.shape[0] // K_CHUNK

    def piece_copies(k):
        columns = pl.ds(k * K_CHUNK, K_CHUNK)
        for p, (ref, (flip, dx, start)) in enumerate(zip(pieces, places)):
            other = lax.rem(x + dx + NX, NX) * 2 + (1 - hi if flip else hi)
            at = pl.multiple_of(other * ROWS + start, 32)
            yield pltpu.make_async_copy(
                ref.at[:, columns], g_all.at[pl.ds(at, ref.shape[0]), columns], g_sem.at[k, p]
            )

    def weight_copy(k):
        rows = pl.ds(k * K_CHUNK, K_CHUNK)
        return pltpu.make_async_copy(weights.at[rows], w_all.at[rows], w_sem.at[k])

    for k in range(chunks):
        weight_copy(k).start()
        for copy in piece_copies(k):
            copy.start()

    tiles = g_all.shape[0] // M_TILE
    for k in range(chunks):
        weight_copy(k).wait()
        for copy in piece_copies(k):
            copy.wait()

        def tile(i, carry, k=k):
            rows = pl.ds(pl.multiple_of(i * M_TILE, M_TILE), M_TILE)
            columns = pl.ds(k * K_CHUNK, K_CHUNK)
            part = jnp.dot(
                g_all[rows, columns], w_all[columns, :], preferred_element_type=jnp.float32
            )
            if k == 0:
                part += adapter_scale * lax.dot_general(
                    projected[rows, :],
                    down[...],
                    (((1,), (1,)), ((), ())),
                    preferred_element_type=jnp.float32,
                )
            else:
                part += total[rows, :]
            if k == chunks - 1:
                out[rows, :] = part.astype(out.dtype)
            else:
                total[rows, :] = part
            return carry

        lax.fori_loop(0, tiles, tile, 0)


def product(pieces, places, weights, projected, down):
    tokens, width = projected.shape[0], weights.shape[1]
    depth = weights.shape[0]
    chunks = depth // K_CHUNK
    whole = pl.BlockSpec(memory_space=pltpu.VMEM)
    outside = pl.BlockSpec(memory_space=pl.ANY)
    return pl.pallas_call(
        functools.partial(product_kernel, places, len(pieces)),
        out_shape=jax.ShapeDtypeStruct((tokens, width), jnp.bfloat16),
        in_specs=[outside] * (len(pieces) + 1) + [whole, whole],
        out_specs=whole,
        scratch_shapes=[
            pltpu.VMEM((tokens, depth), jnp.bfloat16),
            pltpu.VMEM((depth, width), jnp.bfloat16),
            pltpu.VMEM((tokens, width), jnp.float32),
            pltpu.SemaphoreType.DMA((chunks, len(pieces))),
            pltpu.SemaphoreType.DMA((chunks,)),
        ],
        compiler_params=pltpu.CompilerParams(vmem_limit_bytes=40 * 1024 * 1024),
        cost_estimate=pl.CostEstimate(
            flops=2 * tokens * width * depth,
            bytes_accessed=2 * (tokens + width) * depth + 2 * tokens * width,
            transcendentals=0,
        ),
    )(*pieces, weights, projected, down)


def tensor_sum(value):
    value = value + hi_swap(value)
    for partner in ((1, 0, 3, 2), (3, 2, 1, 0)):
        moved = lax.ppermute(
            value, "tensor", [(t, partner[t // 2] * 2 + t % 2) for t in range(2 * NX)]
        )
        value = value + moved
    return value


def body(
    attention_output,
    output_gradient,
    codes,
    block_scale_values,
    adapter_down_factor,
    adapter_up_factor,
):
    f32, bf16 = jnp.float32, jnp.bfloat16
    scale_factor = adapter_scale / loss_scale_factor
    n_dp = lax.axis_size("dp")
    n_tensor = lax.axis_size("tensor")

    scaled = (codes.astype(f32) * jnp.repeat(block_scale_values, BLOCK, axis=0)).astype(bf16)
    weights = lax.all_gather(scaled.T, "dp", axis=0, tiled=True)

    half = ROWS // 2
    other = [hi_swap(output_gradient[:half]), hi_swap(output_gradient[half:])]
    pieces, places = [], []
    for flip, base, own in (
        (0, 0, output_gradient),
        (1, 0, other[0]),
        (1, half, other[1]),
    ):
        for value, dx, start in x_gather(own):
            pieces.append(value)
            places.append((flip, dx, base + start))

    projected_own = lax.dot_general(
        output_gradient, adapter_up_factor, (((1,), (1,)), ((), ())), preferred_element_type=f32
    ).astype(bf16)
    partial_result = jnp.dot(attention_output, adapter_down_factor, preferred_element_type=f32)
    parcel = jnp.concatenate(
        [
            partial_result.reshape(n_tensor, ROWS, -1),
            jnp.broadcast_to(projected_own.astype(f32)[None], (n_tensor,) + projected_own.shape),
        ],
        axis=2,
    )
    parcel = lax.all_to_all(parcel, "tensor", 0, 0, tiled=True)
    rank = adapter_down_factor.shape[1]
    adapted = jnp.sum(parcel[:, :, :rank], axis=0).astype(bf16)
    projected = parcel[:, :, rank:].reshape(n_tensor * ROWS, rank).astype(bf16)

    up_term = lax.dot_general(
        adapted, output_gradient, (((0,), (0,)), ((), ())), preferred_element_type=f32
    )
    down_term = lax.dot_general(
        attention_output, projected, (((0,), (0,)), ((), ())), preferred_element_type=f32
    )
    up_parcel = up_term.reshape(rank, n_dp, -1).transpose(1, 0, 2)
    down_parcel = down_term.reshape(n_dp, -1, up_parcel.shape[2])
    second = lax.all_to_all(
        jnp.concatenate([up_parcel, down_parcel], axis=1), "dp", 0, 0, tiled=True
    )
    summed = scale_factor * jnp.sum(second, axis=0)
    up_factor_gradient = tensor_sum(summed[:rank])
    down_part = summed[rank:]
    down_factor_gradient = lax.all_to_all(
        jnp.broadcast_to(down_part[None], (n_dp,) + down_part.shape), "dp", 0, 0, tiled=True
    ).reshape(-1, rank)

    input_gradient = product(pieces, places, weights, projected, adapter_down_factor)
    return (input_gradient, down_factor_gradient, up_factor_gradient)


def solution(mesh):
    placed = (
        P("dp", "tensor"),
        P(("dp", "tensor"), None),
        P("tensor", "dp"),
        P("tensor", "dp"),
        P("tensor", None),
        P(),
    )
    return jax.shard_map(
        body,
        mesh=mesh,
        in_specs=placed,
        out_specs=(P("dp", "tensor"), P("tensor", None), P(None, "dp")),
        check_vma=False,
    )
```

```python
import functools

import jax
import jax.numpy as jnp
from jax import lax
from jax.experimental import pallas as pl
from jax.experimental.pallas import tpu as pltpu
from jax.sharding import PartitionSpec as P

BLOCK = 128
NX, NY, NZ = 4, 4, 4
STEPS = (0, 1, -1, 2)
ROWS = 128
M_TILE = 256
COST = 40 * 10**9

adapter_scale = 2.0
loss_scale_factor = 64.0


def hi_swap(value):
    return lax.ppermute(value, "tensor", [(t, t ^ 1) for t in range(2 * NX)])


def x_shift(value, step):
    return lax.ppermute(
        value,
        "tensor",
        [(t, ((t // 2 + step) % NX) * 2 + t % 2) for t in range(2 * NX)],
    )


def core_swap(value):
    return lax.ppermute(value, "dp", [(d, d ^ 1) for d in range(2 * NY * NZ)])


def z_shift(value, step):
    pairs = []
    for d in range(2 * NY * NZ):
        y, z, c = d // (2 * NZ), d // 2 % NZ, d % 2
        pairs.append((d, (y * NZ + (z + step) % NZ) * 2 + c))
    return lax.ppermute(value, "dp", pairs)


def y_shift(value, step):
    n = 2 * NY * NZ
    return lax.ppermute(value, "dp", [(d, (d + step * 2 * NZ) % n) for d in range(n)])


def ring_places(flip, base):
    return [(flip, dx, base) for dx in (0, -1, 1, 2)]


def product_kernel(places, sizes, fresh, *refs):
    count = len(places)
    pieces, projected, down = refs[:count], refs[count], refs[count + 1]
    if fresh:
        blocks = refs[count + 2 : count + 2 + 2 * NY]
        out, ordered, *scratch = refs[count + 2 + 2 * NY :]
    else:
        ordered, _, out, *scratch = refs[count + 2 :]
    w_all, g_all, p_all, o_all, w_sem, g_sem, o_sem, h_sem = scratch
    tensor, group = lax.axis_index("tensor"), lax.axis_index("dp")
    x, hi = tensor // 2, lax.rem(tensor, 2)
    y, z, core = group // (2 * NZ), lax.rem(group // 2, NZ), lax.rem(group, 2)
    tokens, depth = g_all.shape
    k_chunk = depth // NY
    starts = [sum(sizes[:p]) for p in range(count)]

    def token(p):
        flip, dx, start = places[p]
        other = lax.rem(x + dx + NX, NX) * 2 + (1 - hi if flip else hi)
        return pl.multiple_of(other * ROWS + start, sizes[p])

    def piece_copy(p):
        return pltpu.make_async_copy(
            pieces[p], g_all.at[pl.ds(starts[p], sizes[p])], g_sem.at[p]
        )

    def weight_rows(k):
        if not fresh:
            return k * k_chunk
        return pl.multiple_of(lax.rem(y + STEPS[k] + NY, NY) * k_chunk, k_chunk)

    def weight_copies(k):
        if not fresh:
            rows = pl.ds(k * k_chunk, k_chunk)
            yield pltpu.make_async_copy(ordered.at[rows], w_all.at[rows], h_sem.at[k])
            return
        for c in range(2):
            for q in range(NZ):
                zz = lax.rem(z + STEPS[q] + NZ, NZ)
                at = weight_rows(k) + (zz * 2 + (1 - core if c else core)) * BLOCK
                yield pltpu.make_async_copy(
                    blocks[2 * k + c].at[pl.ds(q * BLOCK, BLOCK)],
                    w_all.at[pl.ds(pl.multiple_of(at, BLOCK), BLOCK)],
                    w_sem.at[k, c * NZ + q],
                )

    def out_copy(p):
        return pltpu.make_async_copy(
            o_all.at[pl.ds(starts[p], sizes[p])], out.at[pl.ds(token(p), sizes[p])], o_sem.at[p]
        )

    first = [p for p in range(count) if starts[p] < M_TILE]
    for p in first:
        piece_copy(p).start()
    for k in range(NY):
        for copy in weight_copies(k):
            copy.start()
    for p in range(count):
        if p not in first:
            piece_copy(p).start()
        p_all[starts[p] : starts[p] + sizes[p], :] = projected[pl.ds(token(p), sizes[p]), :]

    for tile in range(tokens // M_TILE):
        low, high = tile * M_TILE, (tile + 1) * M_TILE
        rows = slice(low, high)
        inside = [p for p in range(count) if low <= starts[p] < high]
        for p in inside:
            piece_copy(p).wait()
        total = adapter_scale * jnp.dot(
            p_all[rows, :], down[...], preferred_element_type=jnp.float32
        )
        if tile == 0:
            for k in range(NY):
                for copy in weight_copies(k):
                    copy.wait()
                columns = pl.ds(weight_rows(k), k_chunk)
                total += jnp.dot(
                    g_all[rows, columns], w_all[columns, :], preferred_element_type=jnp.float32
                )
            if fresh:
                pltpu.make_async_copy(w_all, ordered, h_sem.at[0]).start()
        else:
            total += jnp.dot(g_all[rows, :], w_all[...], preferred_element_type=jnp.float32)
        o_all[rows, :] = total.astype(o_all.dtype)
        for p in inside:
            out_copy(p).start()
    for p in range(count):
        out_copy(p).wait()
    if fresh:
        pltpu.make_async_copy(w_all, ordered, h_sem.at[0]).wait()


def product(gathered, projected, down, blocks=None, weights=None, held=None):
    pieces = [piece for values, _ in gathered for piece in values]
    places = [place for _, values in gathered for place in values]
    sizes = [piece.shape[0] for piece in pieces]
    tokens, width = sum(sizes), down.shape[1]
    depth, rank = pieces[0].shape[1], projected.shape[1]
    fresh = blocks is not None
    whole = pl.BlockSpec(memory_space=pltpu.VMEM)
    outside = pl.BlockSpec(memory_space=pl.ANY)
    operands = [*pieces, projected, down]
    specs = [outside] * len(pieces) + [whole, whole]
    result = jax.ShapeDtypeStruct((projected.shape[0], width), jnp.bfloat16)
    scratch = [
        pltpu.VMEM((depth, width), jnp.bfloat16),
        pltpu.VMEM((tokens, depth), jnp.bfloat16),
        pltpu.VMEM((tokens, rank), jnp.bfloat16),
        pltpu.VMEM((tokens, width), jnp.bfloat16),
        pltpu.SemaphoreType.DMA((NY, 2 * NZ)),
        pltpu.SemaphoreType.DMA((len(pieces),)),
        pltpu.SemaphoreType.DMA((len(pieces),)),
        pltpu.SemaphoreType.DMA((NY,)),
    ]
    if fresh:
        operands += blocks
        specs += [outside] * len(blocks)
        outs, out_specs = (result, jax.ShapeDtypeStruct((depth, width), jnp.bfloat16)), (outside, outside)
        aliases = {}
    else:
        aliases = {len(operands) + 1: 0}
        operands += [weights, held]
        specs += [outside, outside]
        outs, out_specs = result, outside
    return pl.pallas_call(
        functools.partial(product_kernel, places, sizes, fresh),
        out_shape=outs,
        in_specs=specs,
        out_specs=out_specs,
        input_output_aliases=aliases,
        scratch_shapes=scratch,
        compiler_params=pltpu.CompilerParams(vmem_limit_bytes=56 * 1024 * 1024),
        cost_estimate=pl.CostEstimate(
            flops=4 * tokens * width * depth,
            bytes_accessed=2 * (tokens + width) * depth + 2 * tokens * width,
            transcendentals=0,
        ),
    )(*operands)


def local(kernel, outs, flops, *operands):
    return pl.pallas_call(
        kernel,
        out_shape=outs,
        in_specs=[pl.BlockSpec(memory_space=pltpu.VMEM)] * len(operands),
        out_specs=jax.tree.map(lambda _: pl.BlockSpec(memory_space=pltpu.VMEM), outs),
        compiler_params=pltpu.CompilerParams(vmem_limit_bytes=24 * 1024 * 1024),
        cost_estimate=pl.CostEstimate(flops=flops, bytes_accessed=8 * 2**20, transcendentals=0),
    )(*operands)


def dot(left, right, left_dim, right_dim):
    return lax.dot_general(
        left, right, (((left_dim,), (right_dim,)), ((), ())), preferred_element_type=jnp.float32
    )


def first_kernel(attention, down_t, gradient, up, parcel):
    rank = down_t.shape[0]
    projected = dot(gradient[...], up[...], 1, 1).astype(parcel.dtype)
    partial = dot(attention[...], down_t[...], 1, 1).astype(parcel.dtype)
    for t in range(parcel.shape[0]):
        parcel[t, :, :rank] = partial[t * ROWS : (t + 1) * ROWS]
        parcel[t, :, rank:] = projected


def second_kernel(arrived, attention, gradient, parcel, projected):
    rank = projected.shape[1]
    sources = arrived.shape[0]
    adapted = arrived[0, :, :rank].astype(jnp.float32)
    for t in range(1, sources):
        adapted += arrived[t, :, :rank].astype(jnp.float32)
    for t in range(sources):
        projected[t * ROWS : (t + 1) * ROWS, :] = arrived[t, :, rank:]
    up_term = dot(adapted.astype(gradient.dtype), gradient[...], 0, 0).astype(parcel.dtype)
    down_term = dot(projected[...], attention[...], 0, 0).astype(parcel.dtype)
    across = down_term.shape[1] // 128
    for d in range(parcel.shape[0]):
        parcel[d, :rank, :] = up_term[:, d * 128 : (d + 1) * 128]
        a, b = d // across, d % across
        parcel[d, rank:, :] = down_term[a * 16 : (a + 1) * 16, b * 128 : (b + 1) * 128]


def third_kernel(factor, arrived, up_parcel, down_parcel):
    rank = up_parcel.shape[0]
    total = arrived[0].astype(jnp.float32)
    for d in range(1, arrived.shape[0]):
        total += arrived[d].astype(jnp.float32)
    total *= factor
    up_parcel[...] = total[:rank]
    for d in range(down_parcel.shape[0]):
        down_parcel[d] = total[rank:]


def body(
    attention_output,
    output_gradient,
    codes,
    block_scale_values,
    adapter_down_factor,
    adapter_up_factor,
):
    f32, bf16 = jnp.float32, jnp.bfloat16
    n_dp, n_tensor = lax.axis_size("dp"), lax.axis_size("tensor")
    rank = adapter_down_factor.shape[1]
    down_t = adapter_down_factor.T
    half = ROWS // 2
    stage = lax.optimization_barrier

    scaled = (codes.astype(f32) * jnp.repeat(block_scale_values, BLOCK, axis=0)).astype(bf16).T
    own_before, own_behind = x_shift(output_gradient, 1), x_shift(output_gradient, -1)
    z_blocks = [scaled] + [z_shift(scaled, -step) for step in STEPS[1:]]
    parcel = local(
        first_kernel,
        jax.ShapeDtypeStruct((n_tensor, ROWS, 2 * rank), bf16),
        COST,
        attention_output, down_t, output_gradient, adapter_up_factor,
    )
    parcel = lax.all_to_all(parcel, "tensor", 0, 0, tiled=True)
    mine = jnp.concatenate(z_blocks, axis=0)
    top, bottom, whole = output_gradient[:half], output_gradient[half:], output_gradient

    mine, top, bottom, whole, own_before, own_behind = stage(
        (mine, top, bottom, whole, own_before, own_behind)
    )
    first = hi_swap(top)
    own_far = x_shift(whole, 2)
    y_blocks = [mine] + [y_shift(mine, -step) for step in STEPS[1:3]]
    mine_swapped = core_swap(mine)
    parcel, projected = local(
        second_kernel,
        (
            jax.ShapeDtypeStruct((n_dp, rank + 16, 128), bf16),
            jax.ShapeDtypeStruct((n_tensor * ROWS, rank), bf16),
        ),
        COST,
        parcel, attention_output, output_gradient,
    )
    parcel = lax.all_to_all(parcel, "dp", 0, 0, tiled=True)

    first, own_far, mine, mine_swapped, bottom, projected, *y_blocks = stage(
        (first, own_far, mine, mine_swapped, bottom, projected, *y_blocks)
    )
    second = hi_swap(bottom)
    first_ring = [first, x_shift(first, 1), x_shift(first, -1), x_shift(first, 2)]
    y_blocks.append(y_shift(mine, -STEPS[3]))

    second, *rest = stage((second, *first_ring, *y_blocks))
    first_ring, y_blocks = rest[:4], rest[4:]
    blocks = [y_blocks[0], mine_swapped]
    for block in y_blocks[1:]:
        blocks += [block, core_swap(block)]
    second_ring = [second, x_shift(second, 1), x_shift(second, -1), x_shift(second, 2)]
    own_ring = [output_gradient, own_before, own_behind, own_far]
    input_gradient, weights = product(
        [(own_ring, ring_places(0, 0)), (first_ring, ring_places(1, 0))],
        projected, down_t, blocks=blocks,
    )
    parcel, input_gradient = stage((parcel, input_gradient))
    up_parcel, down_parcel = local(
        functools.partial(third_kernel, adapter_scale / loss_scale_factor),
        (
            jax.ShapeDtypeStruct((rank, 128), f32),
            jax.ShapeDtypeStruct((n_dp, 16, 128), f32),
        ),
        10**8,
        parcel,
    )
    down_parcel = lax.all_to_all(down_parcel, "dp", 0, 0, tiled=True)
    up_part = (up_parcel + x_shift(up_parcel, 2)) + (
        x_shift(up_parcel, 1) + x_shift(up_parcel, -1)
    )

    up_part, input_gradient, *second_ring = stage((up_part, input_gradient, *second_ring))
    up_factor_gradient = up_part + hi_swap(up_part)
    down_factor_gradient = (
        down_parcel.reshape(rank // 16, -1, 16, 128).transpose(0, 2, 1, 3).reshape(rank, -1).T
    )
    input_gradient = product(
        [(second_ring, ring_places(1, half))],
        projected, down_t, weights=weights, held=input_gradient,
    )
    return (input_gradient, down_factor_gradient, up_factor_gradient)


def solution(mesh):
    placed = (
        P("dp", "tensor"),
        P(("dp", "tensor"), None),
        P("tensor", "dp"),
        P("tensor", "dp"),
        P("tensor", None),
        P(),
    )
    return jax.shard_map(
        body,
        mesh=mesh,
        in_specs=placed,
        out_specs=(P("dp", "tensor"), P("tensor", None), P(None, "dp")),
        check_vma=False,
    )
```

```python
import functools

import jax
import jax.numpy as jnp
from jax import lax
from jax.experimental import pallas as pl
from jax.experimental.pallas import tpu as pltpu
from jax.sharding import PartitionSpec as P

BLOCK = 128
NX, NY, NZ = 4, 4, 4
STEPS = (0, 1, -1, 2)
ROWS = 128
M_TILE = 256
COST = 40 * 10**9

adapter_scale = 2.0
loss_scale_factor = 64.0


def hi_swap(value):
    return lax.ppermute(value, "tensor", [(t, t ^ 1) for t in range(2 * NX)])


def x_shift(value, step):
    return lax.ppermute(
        value,
        "tensor",
        [(t, ((t // 2 + step) % NX) * 2 + t % 2) for t in range(2 * NX)],
    )


def core_swap(value):
    return lax.ppermute(value, "dp", [(d, d ^ 1) for d in range(2 * NY * NZ)])


def z_shift(value, step):
    pairs = []
    for d in range(2 * NY * NZ):
        y, z, c = d // (2 * NZ), d // 2 % NZ, d % 2
        pairs.append((d, (y * NZ + (z + step) % NZ) * 2 + c))
    return lax.ppermute(value, "dp", pairs)


def y_shift(value, step):
    n = 2 * NY * NZ
    return lax.ppermute(value, "dp", [(d, (d + step * 2 * NZ) % n) for d in range(n)])


def ring_places(flip, base):
    return [(flip, dx, base) for dx in (0, -1, 1, 2)]


def product_kernel(places, sizes, fresh, *refs):
    count = len(places)
    pieces, projected, down = refs[:count], refs[count], refs[count + 1]
    if fresh:
        blocks = refs[count + 2 : count + 2 + 2 * NY]
        out, ordered, *scratch = refs[count + 2 + 2 * NY :]
    else:
        ordered, _, out, *scratch = refs[count + 2 :]
    w_all, g_all, p_all, o_all, w_sem, g_sem, o_sem, h_sem = scratch
    tensor, group = lax.axis_index("tensor"), lax.axis_index("dp")
    x, hi = tensor // 2, lax.rem(tensor, 2)
    y, z, core = group // (2 * NZ), lax.rem(group // 2, NZ), lax.rem(group, 2)
    tokens, depth = g_all.shape
    k_chunk = depth // NY
    starts = [sum(sizes[:p]) for p in range(count)]

    def token(p):
        flip, dx, start = places[p]
        other = lax.rem(x + dx + NX, NX) * 2 + (1 - hi if flip else hi)
        return pl.multiple_of(other * ROWS + start, sizes[p])

    def piece_copy(p):
        return pltpu.make_async_copy(
            pieces[p], g_all.at[pl.ds(starts[p], sizes[p])], g_sem.at[p]
        )

    def weight_rows(k):
        if not fresh:
            return k * k_chunk
        return pl.multiple_of(lax.rem(y + STEPS[k] + NY, NY) * k_chunk, k_chunk)

    def weight_copies(k):
        if not fresh:
            rows = pl.ds(k * k_chunk, k_chunk)
            yield pltpu.make_async_copy(ordered.at[rows], w_all.at[rows], h_sem.at[k])
            return
        for c in range(2):
            for q in range(NZ):
                zz = lax.rem(z + STEPS[q] + NZ, NZ)
                at = weight_rows(k) + (zz * 2 + (1 - core if c else core)) * BLOCK
                yield pltpu.make_async_copy(
                    blocks[2 * k + c].at[pl.ds(q * BLOCK, BLOCK)],
                    w_all.at[pl.ds(pl.multiple_of(at, BLOCK), BLOCK)],
                    w_sem.at[k, c * NZ + q],
                )

    def out_copy(p):
        return pltpu.make_async_copy(
            o_all.at[pl.ds(starts[p], sizes[p])], out.at[pl.ds(token(p), sizes[p])], o_sem.at[p]
        )

    first = [p for p in range(count) if starts[p] < M_TILE]
    for p in first:
        piece_copy(p).start()
    for k in range(NY):
        for copy in weight_copies(k):
            copy.start()
    for p in range(count):
        if p not in first:
            piece_copy(p).start()
        p_all[starts[p] : starts[p] + sizes[p], :] = projected[pl.ds(token(p), sizes[p]), :]

    for tile in range(tokens // M_TILE):
        low, high = tile * M_TILE, (tile + 1) * M_TILE
        rows = slice(low, high)
        inside = [p for p in range(count) if low <= starts[p] < high]
        for p in inside:
            piece_copy(p).wait()
        total = adapter_scale * jnp.dot(
            p_all[rows, :], down[...], preferred_element_type=jnp.float32
        )
        if tile == 0:
            for k in range(NY):
                for copy in weight_copies(k):
                    copy.wait()
                columns = pl.ds(weight_rows(k), k_chunk)
                total += jnp.dot(
                    g_all[rows, columns], w_all[columns, :], preferred_element_type=jnp.float32
                )
            if fresh:
                pltpu.make_async_copy(w_all, ordered, h_sem.at[0]).start()
        else:
            total += jnp.dot(g_all[rows, :], w_all[...], preferred_element_type=jnp.float32)
        o_all[rows, :] = total.astype(o_all.dtype)
        for p in inside:
            out_copy(p).start()
    for p in range(count):
        out_copy(p).wait()
    if fresh:
        pltpu.make_async_copy(w_all, ordered, h_sem.at[0]).wait()


def product(gathered, projected, down, blocks=None, weights=None, held=None):
    pieces = [piece for values, _ in gathered for piece in values]
    places = [place for _, values in gathered for place in values]
    sizes = [piece.shape[0] for piece in pieces]
    tokens, width = sum(sizes), down.shape[1]
    depth, rank = pieces[0].shape[1], projected.shape[1]
    fresh = blocks is not None
    whole = pl.BlockSpec(memory_space=pltpu.VMEM)
    outside = pl.BlockSpec(memory_space=pl.ANY)
    operands = [*pieces, projected, down]
    specs = [outside] * len(pieces) + [whole, whole]
    result = jax.ShapeDtypeStruct((projected.shape[0], width), jnp.bfloat16)
    scratch = [
        pltpu.VMEM((depth, width), jnp.bfloat16),
        pltpu.VMEM((tokens, depth), jnp.bfloat16),
        pltpu.VMEM((tokens, rank), jnp.bfloat16),
        pltpu.VMEM((tokens, width), jnp.bfloat16),
        pltpu.SemaphoreType.DMA((NY, 2 * NZ)),
        pltpu.SemaphoreType.DMA((len(pieces),)),
        pltpu.SemaphoreType.DMA((len(pieces),)),
        pltpu.SemaphoreType.DMA((NY,)),
    ]
    if fresh:
        operands += blocks
        specs += [outside] * len(blocks)
        outs, out_specs = (result, jax.ShapeDtypeStruct((depth, width), jnp.bfloat16)), (outside, outside)
        aliases = {}
    else:
        aliases = {len(operands) + 1: 0}
        operands += [weights, held]
        specs += [outside, outside]
        outs, out_specs = result, outside
    return pl.pallas_call(
        functools.partial(product_kernel, places, sizes, fresh),
        out_shape=outs,
        in_specs=specs,
        out_specs=out_specs,
        input_output_aliases=aliases,
        scratch_shapes=scratch,
        compiler_params=pltpu.CompilerParams(vmem_limit_bytes=56 * 1024 * 1024),
        cost_estimate=pl.CostEstimate(
            flops=4 * tokens * width * depth,
            bytes_accessed=2 * (tokens + width) * depth + 2 * tokens * width,
            transcendentals=0,
        ),
    )(*operands)


def last_kernel(places, *refs):
    count = len(places)
    pieces = refs[:count]
    projected, down, weights, _, out, o_all, o_sem = refs[count:]
    tensor = lax.axis_index("tensor")
    x, hi = tensor // 2, lax.rem(tensor, 2)
    size = pieces[0].shape[0]

    def token(p):
        flip, dx, start = places[p]
        other = lax.rem(x + dx + NX, NX) * 2 + (1 - hi if flip else hi)
        return pl.multiple_of(other * ROWS + start, size)

    rows = jnp.concatenate([piece[...] for piece in pieces], axis=0)
    narrow = jnp.concatenate([projected[pl.ds(token(p), size), :] for p in range(count)], axis=0)
    total = adapter_scale * jnp.dot(narrow, down[...], preferred_element_type=jnp.float32)
    total += jnp.dot(rows, weights[...], preferred_element_type=jnp.float32)
    o_all[...] = total.astype(o_all.dtype)
    copies = [
        pltpu.make_async_copy(
            o_all.at[pl.ds(p * size, size)], out.at[pl.ds(token(p), size)], o_sem.at[p]
        )
        for p in range(count)
    ]
    for copy in copies:
        copy.start()
    for copy in copies:
        copy.wait()


def last_product(gathered, projected, down, weights, held):
    (pieces, places), = gathered
    tokens, width = pieces[0].shape[0] * len(pieces), down.shape[1]
    depth = pieces[0].shape[1]
    whole = pl.BlockSpec(memory_space=pltpu.VMEM)
    outside = pl.BlockSpec(memory_space=pl.ANY)
    operands = [*pieces, projected, down, weights, held]
    return pl.pallas_call(
        functools.partial(last_kernel, places),
        out_shape=jax.ShapeDtypeStruct(held.shape, held.dtype),
        in_specs=[whole] * (len(operands) - 1) + [outside],
        out_specs=outside,
        input_output_aliases={len(operands) - 1: 0},
        scratch_shapes=[
            pltpu.VMEM((tokens, width), held.dtype),
            pltpu.SemaphoreType.DMA((len(pieces),)),
        ],
        compiler_params=pltpu.CompilerParams(vmem_limit_bytes=24 * 1024 * 1024),
        cost_estimate=pl.CostEstimate(
            flops=2 * tokens * width * depth,
            bytes_accessed=2 * (tokens + width) * depth + 2 * tokens * width,
            transcendentals=0,
        ),
    )(*operands)


def local(kernel, outs, flops, *operands):
    return pl.pallas_call(
        kernel,
        out_shape=outs,
        in_specs=[pl.BlockSpec(memory_space=pltpu.VMEM)] * len(operands),
        out_specs=jax.tree.map(lambda _: pl.BlockSpec(memory_space=pltpu.VMEM), outs),
        compiler_params=pltpu.CompilerParams(vmem_limit_bytes=24 * 1024 * 1024),
        cost_estimate=pl.CostEstimate(flops=flops, bytes_accessed=8 * 2**20, transcendentals=0),
    )(*operands)


def dot(left, right, left_dim, right_dim):
    return lax.dot_general(
        left, right, (((left_dim,), (right_dim,)), ((), ())), preferred_element_type=jnp.float32
    )


def first_kernel(attention, down_t, gradient, up, parcel):
    rank = down_t.shape[0]
    half = ROWS // 2
    projected = dot(gradient[...], up[...], 1, 1).astype(parcel.dtype)
    partial = dot(attention[...], down_t[...], 1, 1)
    high = partial.astype(parcel.dtype)
    low = (partial - high.astype(jnp.float32)).astype(parcel.dtype)
    for t in range(parcel.shape[0]):
        parcel[t, :ROWS, :rank] = high[t * ROWS : (t + 1) * ROWS]
        parcel[t, :ROWS, rank:] = low[t * ROWS : (t + 1) * ROWS]
        parcel[t, ROWS:, :rank] = projected[:half]
        parcel[t, ROWS:, rank:] = projected[half:]


def second_kernel(arrived, attention, gradient, parcel, projected):
    rank = projected.shape[1]
    sources = arrived.shape[0]
    half = ROWS // 2
    sums = arrived[0, :ROWS].astype(jnp.float32)
    for t in range(1, sources):
        sums += arrived[t, :ROWS].astype(jnp.float32)
    adapted = sums[:, :rank] + sums[:, rank:]
    for t in range(sources):
        projected[t * ROWS : t * ROWS + half, :] = arrived[t, ROWS:, :rank]
        projected[t * ROWS + half : (t + 1) * ROWS, :] = arrived[t, ROWS:, rank:]
    up_term = dot(adapted.astype(gradient.dtype), gradient[...], 0, 0).astype(parcel.dtype)
    down_term = dot(projected[...], attention[...], 0, 0).astype(parcel.dtype)
    across = down_term.shape[1] // 128
    for d in range(parcel.shape[0]):
        parcel[d, :rank, :] = up_term[:, d * 128 : (d + 1) * 128]
        a, b = d // across, d % across
        parcel[d, rank:, :] = down_term[a * 16 : (a + 1) * 16, b * 128 : (b + 1) * 128]


def third_kernel(factor, arrived, up_parcel, down_parcel):
    rank = up_parcel.shape[0]
    total = arrived[0].astype(jnp.float32)
    for d in range(1, arrived.shape[0]):
        total += arrived[d].astype(jnp.float32)
    total *= factor
    up_parcel[...] = total[:rank]
    for d in range(down_parcel.shape[0]):
        down_parcel[d] = total[rank:]


def body(
    attention_output,
    output_gradient,
    codes,
    block_scale_values,
    adapter_down_factor,
    adapter_up_factor,
):
    f32, bf16 = jnp.float32, jnp.bfloat16
    n_dp, n_tensor = lax.axis_size("dp"), lax.axis_size("tensor")
    rank = adapter_down_factor.shape[1]
    down_t = adapter_down_factor.T
    half = ROWS // 2
    stage = lax.optimization_barrier

    scaled = (codes.astype(f32) * jnp.repeat(block_scale_values, BLOCK, axis=0)).astype(bf16).T
    own_before, own_behind = x_shift(output_gradient, 1), x_shift(output_gradient, -1)
    z_blocks = [scaled] + [z_shift(scaled, -step) for step in STEPS[1:]]
    parcel = local(
        first_kernel,
        jax.ShapeDtypeStruct((n_tensor, ROWS + ROWS // 2, 2 * rank), bf16),
        COST,
        attention_output, down_t, output_gradient, adapter_up_factor,
    )
    parcel = lax.all_to_all(parcel, "tensor", 0, 0, tiled=True)
    mine = jnp.concatenate(z_blocks, axis=0)
    top, bottom, whole = output_gradient[:half], output_gradient[half:], output_gradient

    mine, top, bottom, whole, own_before, own_behind = stage(
        (mine, top, bottom, whole, own_before, own_behind)
    )
    first = hi_swap(top)
    own_far = x_shift(whole, 2)
    y_blocks = [mine] + [y_shift(mine, -step) for step in STEPS[1:3]]
    mine_swapped = core_swap(mine)
    parcel, projected = local(
        second_kernel,
        (
            jax.ShapeDtypeStruct((n_dp, rank + 16, 128), bf16),
            jax.ShapeDtypeStruct((n_tensor * ROWS, rank), bf16),
        ),
        COST,
        parcel, attention_output, output_gradient,
    )
    parcel = lax.all_to_all(parcel, "dp", 0, 0, tiled=True)

    first, own_far, mine, mine_swapped, bottom, projected, *y_blocks = stage(
        (first, own_far, mine, mine_swapped, bottom, projected, *y_blocks)
    )
    second = hi_swap(bottom)
    first_ring = [first, x_shift(first, 1), x_shift(first, -1), x_shift(first, 2)]
    y_blocks.append(y_shift(mine, -STEPS[3]))

    second, *rest = stage((second, *first_ring, *y_blocks))
    first_ring, y_blocks = rest[:4], rest[4:]
    blocks = [y_blocks[0], mine_swapped]
    for block in y_blocks[1:]:
        blocks += [block, core_swap(block)]
    second_ring = [second, x_shift(second, 1), x_shift(second, -1), x_shift(second, 2)]
    own_ring = [output_gradient, own_before, own_behind, own_far]
    input_gradient, weights = product(
        [(own_ring, ring_places(0, 0)), (first_ring, ring_places(1, 0))],
        projected, down_t, blocks=blocks,
    )
    parcel, input_gradient = stage((parcel, input_gradient))
    up_parcel, down_parcel = local(
        functools.partial(third_kernel, adapter_scale / loss_scale_factor),
        (
            jax.ShapeDtypeStruct((rank, 128), f32),
            jax.ShapeDtypeStruct((n_dp, 16, 128), f32),
        ),
        10**8,
        parcel,
    )
    down_parcel = lax.all_to_all(down_parcel, "dp", 0, 0, tiled=True)
    up_part = (up_parcel + x_shift(up_parcel, 2)) + (
        x_shift(up_parcel, 1) + x_shift(up_parcel, -1)
    )

    up_part, input_gradient, *second_ring = stage((up_part, input_gradient, *second_ring))
    up_factor_gradient = up_part + hi_swap(up_part)
    down_factor_gradient = (
        down_parcel.reshape(rank // 16, -1, 16, 128).transpose(0, 2, 1, 3).reshape(rank, -1).T
    )
    input_gradient = last_product(
        [(second_ring, ring_places(1, half))],
        projected, down_t, weights=weights, held=input_gradient,
    )
    return (input_gradient, down_factor_gradient, up_factor_gradient)


def solution(mesh):
    placed = (
        P("dp", "tensor"),
        P(("dp", "tensor"), None),
        P("tensor", "dp"),
        P("tensor", "dp"),
        P("tensor", None),
        P(),
    )
    return jax.shard_map(
        body,
        mesh=mesh,
        in_specs=placed,
        out_specs=(P("dp", "tensor"), P("tensor", None), P(None, "dp")),
        check_vma=False,
    )
```

```python
import functools

import jax
import jax.numpy as jnp
from jax import lax
from jax.experimental import pallas as pl
from jax.experimental.pallas import tpu as pltpu
from jax.sharding import PartitionSpec as P

BLOCK = 128
NX, NY, NZ = 4, 4, 4
STEPS = (0, 1, -1, 2)
ROWS = 128
M_TILE = 256
COST = 40 * 10**9

adapter_scale = 2.0
loss_scale_factor = 64.0


def hi_swap(value):
    return lax.ppermute(value, "tensor", [(t, t ^ 1) for t in range(2 * NX)])


def x_shift(value, step):
    return lax.ppermute(
        value,
        "tensor",
        [(t, ((t // 2 + step) % NX) * 2 + t % 2) for t in range(2 * NX)],
    )


def core_swap(value):
    return lax.ppermute(value, "dp", [(d, d ^ 1) for d in range(2 * NY * NZ)])


def z_shift(value, step):
    pairs = []
    for d in range(2 * NY * NZ):
        y, z, c = d // (2 * NZ), d // 2 % NZ, d % 2
        pairs.append((d, (y * NZ + (z + step) % NZ) * 2 + c))
    return lax.ppermute(value, "dp", pairs)


def y_shift(value, step):
    n = 2 * NY * NZ
    return lax.ppermute(value, "dp", [(d, (d + step * 2 * NZ) % n) for d in range(n)])


def ring_places(flip, base):
    return [(flip, dx, base) for dx in (0, -1, 1, 2)]


def product_kernel(places, sizes, fresh, *refs):
    count = len(places)
    pieces, projected, down = refs[:count], refs[count], refs[count + 1]
    if fresh:
        blocks = refs[count + 2 : count + 2 + 2 * NY]
        out, ordered, *scratch = refs[count + 2 + 2 * NY :]
    else:
        ordered, _, out, *scratch = refs[count + 2 :]
    w_all, g_all, p_all, o_all, w_sem, g_sem, o_sem, h_sem = scratch
    tensor, group = lax.axis_index("tensor"), lax.axis_index("dp")
    x, hi = tensor // 2, lax.rem(tensor, 2)
    y, z, core = group // (2 * NZ), lax.rem(group // 2, NZ), lax.rem(group, 2)
    tokens, depth = g_all.shape
    k_chunk = depth // NY
    starts = [sum(sizes[:p]) for p in range(count)]

    def token(p):
        flip, dx, start = places[p]
        other = lax.rem(x + dx + NX, NX) * 2 + (1 - hi if flip else hi)
        return pl.multiple_of(other * ROWS + start, sizes[p])

    def piece_copy(p):
        return pltpu.make_async_copy(
            pieces[p], g_all.at[pl.ds(starts[p], sizes[p])], g_sem.at[p]
        )

    def weight_rows(k):
        if not fresh:
            return k * k_chunk
        return pl.multiple_of(lax.rem(y + STEPS[k] + NY, NY) * k_chunk, k_chunk)

    def weight_copies(k):
        if not fresh:
            rows = pl.ds(k * k_chunk, k_chunk)
            yield pltpu.make_async_copy(ordered.at[rows], w_all.at[rows], h_sem.at[k])
            return
        for c in range(2):
            for q in range(NZ):
                zz = lax.rem(z + STEPS[q] + NZ, NZ)
                at = weight_rows(k) + (zz * 2 + (1 - core if c else core)) * BLOCK
                yield pltpu.make_async_copy(
                    blocks[2 * k + c].at[pl.ds(q * BLOCK, BLOCK)],
                    w_all.at[pl.ds(pl.multiple_of(at, BLOCK), BLOCK)],
                    w_sem.at[k, c * NZ + q],
                )

    def out_copy(p):
        return pltpu.make_async_copy(
            o_all.at[pl.ds(starts[p], sizes[p])], out.at[pl.ds(token(p), sizes[p])], o_sem.at[p]
        )

    first = [p for p in range(count) if starts[p] < M_TILE]
    for p in first:
        piece_copy(p).start()
    for k in range(NY):
        for copy in weight_copies(k):
            copy.start()
    for p in range(count):
        if p not in first:
            piece_copy(p).start()
        p_all[starts[p] : starts[p] + sizes[p], :] = projected[pl.ds(token(p), sizes[p]), :]

    for tile in range(tokens // M_TILE):
        low, high = tile * M_TILE, (tile + 1) * M_TILE
        rows = slice(low, high)
        inside = [p for p in range(count) if low <= starts[p] < high]
        for p in inside:
            piece_copy(p).wait()
        total = adapter_scale * jnp.dot(
            p_all[rows, :], down[...], preferred_element_type=jnp.float32
        )
        if tile == 0:
            for k in range(NY):
                for copy in weight_copies(k):
                    copy.wait()
                columns = pl.ds(weight_rows(k), k_chunk)
                total += jnp.dot(
                    g_all[rows, columns], w_all[columns, :], preferred_element_type=jnp.float32
                )
            if fresh:
                pltpu.make_async_copy(w_all, ordered, h_sem.at[0]).start()
        else:
            total += jnp.dot(g_all[rows, :], w_all[...], preferred_element_type=jnp.float32)
        o_all[rows, :] = total.astype(o_all.dtype)
        for p in inside:
            out_copy(p).start()
    for p in range(count):
        out_copy(p).wait()
    if fresh:
        pltpu.make_async_copy(w_all, ordered, h_sem.at[0]).wait()


def product(gathered, projected, down, blocks=None, weights=None, held=None):
    pieces = [piece for values, _ in gathered for piece in values]
    places = [place for _, values in gathered for place in values]
    sizes = [piece.shape[0] for piece in pieces]
    tokens, width = sum(sizes), down.shape[1]
    depth, rank = pieces[0].shape[1], projected.shape[1]
    fresh = blocks is not None
    whole = pl.BlockSpec(memory_space=pltpu.VMEM)
    outside = pl.BlockSpec(memory_space=pl.ANY)
    operands = [*pieces, projected, down]
    specs = [outside] * len(pieces) + [whole, whole]
    result = jax.ShapeDtypeStruct((projected.shape[0], width), jnp.bfloat16)
    scratch = [
        pltpu.VMEM((depth, width), jnp.bfloat16),
        pltpu.VMEM((tokens, depth), jnp.bfloat16),
        pltpu.VMEM((tokens, rank), jnp.bfloat16),
        pltpu.VMEM((tokens, width), jnp.bfloat16),
        pltpu.SemaphoreType.DMA((NY, 2 * NZ)),
        pltpu.SemaphoreType.DMA((len(pieces),)),
        pltpu.SemaphoreType.DMA((len(pieces),)),
        pltpu.SemaphoreType.DMA((NY,)),
    ]
    if fresh:
        operands += blocks
        specs += [outside] * len(blocks)
        outs, out_specs = (result, jax.ShapeDtypeStruct((depth, width), jnp.bfloat16)), (outside, outside)
        aliases = {}
    else:
        aliases = {len(operands) + 1: 0}
        operands += [weights, held]
        specs += [outside, outside]
        outs, out_specs = result, outside
    return pl.pallas_call(
        functools.partial(product_kernel, places, sizes, fresh),
        out_shape=outs,
        in_specs=specs,
        out_specs=out_specs,
        input_output_aliases=aliases,
        scratch_shapes=scratch,
        compiler_params=pltpu.CompilerParams(vmem_limit_bytes=56 * 1024 * 1024),
        cost_estimate=pl.CostEstimate(
            flops=4 * tokens * width * depth,
            bytes_accessed=2 * (tokens + width) * depth + 2 * tokens * width,
            transcendentals=0,
        ),
    )(*operands)


def last_kernel(places, *refs):
    count = len(places)
    pieces = refs[:count]
    projected, down, weights, _, out, o_all, o_sem = refs[count:]
    tensor = lax.axis_index("tensor")
    x, hi = tensor // 2, lax.rem(tensor, 2)
    size = pieces[0].shape[0]

    def token(p):
        flip, dx, start = places[p]
        other = lax.rem(x + dx + NX, NX) * 2 + (1 - hi if flip else hi)
        return pl.multiple_of(other * ROWS + start, size)

    rows = jnp.concatenate([piece[...] for piece in pieces], axis=0)
    narrow = jnp.concatenate([projected[pl.ds(token(p), size), :] for p in range(count)], axis=0)
    total = adapter_scale * jnp.dot(narrow, down[...], preferred_element_type=jnp.float32)
    total += jnp.dot(rows, weights[...], preferred_element_type=jnp.float32)
    o_all[...] = total.astype(o_all.dtype)
    copies = [
        pltpu.make_async_copy(
            o_all.at[pl.ds(p * size, size)], out.at[pl.ds(token(p), size)], o_sem.at[p]
        )
        for p in range(count)
    ]
    for copy in copies:
        copy.start()
    for copy in copies:
        copy.wait()


def last_product(gathered, projected, down, weights, held):
    (pieces, places), = gathered
    tokens, width = pieces[0].shape[0] * len(pieces), down.shape[1]
    depth = pieces[0].shape[1]
    whole = pl.BlockSpec(memory_space=pltpu.VMEM)
    outside = pl.BlockSpec(memory_space=pl.ANY)
    operands = [*pieces, projected, down, weights, held]
    return pl.pallas_call(
        functools.partial(last_kernel, places),
        out_shape=jax.ShapeDtypeStruct(held.shape, held.dtype),
        in_specs=[whole] * (len(operands) - 1) + [outside],
        out_specs=outside,
        input_output_aliases={len(operands) - 1: 0},
        scratch_shapes=[
            pltpu.VMEM((tokens, width), held.dtype),
            pltpu.SemaphoreType.DMA((len(pieces),)),
        ],
        compiler_params=pltpu.CompilerParams(vmem_limit_bytes=24 * 1024 * 1024),
        cost_estimate=pl.CostEstimate(
            flops=2 * tokens * width * depth,
            bytes_accessed=2 * (tokens + width) * depth + 2 * tokens * width,
            transcendentals=0,
        ),
    )(*operands)


def local(kernel, outs, flops, *operands):
    return pl.pallas_call(
        kernel,
        out_shape=outs,
        in_specs=[pl.BlockSpec(memory_space=pltpu.VMEM)] * len(operands),
        out_specs=jax.tree.map(lambda _: pl.BlockSpec(memory_space=pltpu.VMEM), outs),
        compiler_params=pltpu.CompilerParams(vmem_limit_bytes=24 * 1024 * 1024),
        cost_estimate=pl.CostEstimate(flops=flops, bytes_accessed=8 * 2**20, transcendentals=0),
    )(*operands)


def dot(left, right, left_dim, right_dim):
    return lax.dot_general(
        left, right, (((left_dim,), (right_dim,)), ((), ())), preferred_element_type=jnp.float32
    )


def first_kernel(attention, down_t, gradient, up, parcel):
    rank = down_t.shape[0]
    half = ROWS // 2
    projected = dot(gradient[...], up[...], 1, 1).astype(parcel.dtype)
    partial = dot(attention[...], down_t[...], 1, 1)
    high = partial.astype(parcel.dtype)
    low = (partial - high.astype(jnp.float32)).astype(parcel.dtype)
    for t in range(parcel.shape[0]):
        parcel[t, :ROWS, :rank] = high[t * ROWS : (t + 1) * ROWS]
        parcel[t, :ROWS, rank:] = low[t * ROWS : (t + 1) * ROWS]
        parcel[t, ROWS:, :rank] = projected[:half]
        parcel[t, ROWS:, rank:] = projected[half:]


def second_kernel(arrived, attention, gradient, parcel, projected):
    rank = projected.shape[1]
    sources = arrived.shape[0]
    half = ROWS // 2
    sums = arrived[0, :ROWS].astype(jnp.float32)
    for t in range(1, sources):
        sums += arrived[t, :ROWS].astype(jnp.float32)
    adapted = sums[:, :rank] + sums[:, rank:]
    for t in range(sources):
        projected[t * ROWS : t * ROWS + half, :] = arrived[t, ROWS:, :rank]
        projected[t * ROWS + half : (t + 1) * ROWS, :] = arrived[t, ROWS:, rank:]
    up_term = dot(adapted.astype(gradient.dtype), gradient[...], 0, 0).astype(parcel.dtype)
    down_term = dot(projected[...], attention[...], 0, 0).astype(parcel.dtype)
    across = down_term.shape[1] // 128
    for d in range(parcel.shape[0]):
        parcel[d, :rank, :] = up_term[:, d * 128 : (d + 1) * 128]
        a, b = d // across, d % across
        parcel[d, rank:, :] = down_term[a * 16 : (a + 1) * 16, b * 128 : (b + 1) * 128]


def third_kernel(factor, arrived, up_parcel, down_parcel):
    rank = up_parcel.shape[0]
    total = arrived[0].astype(jnp.float32)
    for d in range(1, arrived.shape[0]):
        total += arrived[d].astype(jnp.float32)
    total *= factor
    up_parcel[...] = total[:rank]
    for d in range(down_parcel.shape[0]):
        down_parcel[d] = total[rank:]


def body(
    attention_output,
    output_gradient,
    codes,
    block_scale_values,
    adapter_down_factor,
    adapter_up_factor,
):
    f32, bf16 = jnp.float32, jnp.bfloat16
    n_dp, n_tensor = lax.axis_size("dp"), lax.axis_size("tensor")
    rank = adapter_down_factor.shape[1]
    down_t = adapter_down_factor.T
    half = ROWS // 2
    stage = lax.optimization_barrier

    scaled = (codes.astype(f32) * jnp.repeat(block_scale_values, BLOCK, axis=0)).astype(bf16).T
    own_before, own_behind = x_shift(output_gradient, 1), x_shift(output_gradient, -1)
    z_blocks = [scaled] + [z_shift(scaled, -step) for step in STEPS[1:]]
    parcel = local(
        first_kernel,
        jax.ShapeDtypeStruct((n_tensor, ROWS + ROWS // 2, 2 * rank), bf16),
        COST,
        attention_output, down_t, output_gradient, adapter_up_factor,
    )
    parcel = lax.all_to_all(parcel, "tensor", 0, 0, tiled=True)
    mine = jnp.concatenate(z_blocks, axis=0)
    top, bottom, whole = output_gradient[:half], output_gradient[half:], output_gradient

    mine, top, bottom, whole, own_before, own_behind = stage(
        (mine, top, bottom, whole, own_before, own_behind)
    )
    first = hi_swap(top)
    own_far = x_shift(whole, 2)
    y_blocks = [mine] + [y_shift(mine, -step) for step in STEPS[1:3]]
    mine_swapped = core_swap(mine)
    parcel, projected = local(
        second_kernel,
        (
            jax.ShapeDtypeStruct((n_dp, rank + 16, 128), bf16),
            jax.ShapeDtypeStruct((n_tensor * ROWS, rank), bf16),
        ),
        COST,
        parcel, attention_output, output_gradient,
    )
    parcel = lax.all_to_all(parcel, "dp", 0, 0, tiled=True)

    first, own_far, mine, mine_swapped, bottom, projected, *y_blocks = stage(
        (first, own_far, mine, mine_swapped, bottom, projected, *y_blocks)
    )
    second = hi_swap(bottom)
    first_ring = [first, x_shift(first, 1), x_shift(first, -1), x_shift(first, 2)]
    y_blocks.append(y_shift(mine, -STEPS[3]))
    up_parcel, down_parcel = local(
        functools.partial(third_kernel, adapter_scale / loss_scale_factor),
        (
            jax.ShapeDtypeStruct((rank, 128), f32),
            jax.ShapeDtypeStruct((n_dp, 16, 128), f32),
        ),
        COST,
        parcel,
    )

    second, *rest = stage((second, *first_ring, *y_blocks))
    first_ring, y_blocks = rest[:4], rest[4:]
    blocks = [y_blocks[0], mine_swapped]
    for block in y_blocks[1:]:
        blocks += [block, core_swap(block)]
    second_ring = [second, x_shift(second, 1), x_shift(second, -1), x_shift(second, 2)]
    own_ring = [output_gradient, own_before, own_behind, own_far]
    input_gradient, weights = product(
        [(own_ring, ring_places(0, 0)), (first_ring, ring_places(1, 0))],
        projected, down_t, blocks=blocks,
    )
    up_parcel, down_parcel, input_gradient = stage((up_parcel, down_parcel, input_gradient))
    down_parcel = lax.all_to_all(down_parcel, "dp", 0, 0, tiled=True)
    up_part = (up_parcel + x_shift(up_parcel, 2)) + (
        x_shift(up_parcel, 1) + x_shift(up_parcel, -1)
    )

    up_part, input_gradient, *second_ring = stage((up_part, input_gradient, *second_ring))
    up_factor_gradient = up_part + hi_swap(up_part)
    down_factor_gradient = (
        down_parcel.reshape(rank // 16, -1, 16, 128).transpose(0, 2, 1, 3).reshape(rank, -1).T
    )
    input_gradient = last_product(
        [(second_ring, ring_places(1, half))],
        projected, down_t, weights=weights, held=input_gradient,
    )
    return (input_gradient, down_factor_gradient, up_factor_gradient)


def solution(mesh):
    placed = (
        P("dp", "tensor"),
        P(("dp", "tensor"), None),
        P("tensor", "dp"),
        P("tensor", "dp"),
        P("tensor", None),
        P(),
    )
    return jax.shard_map(
        body,
        mesh=mesh,
        in_specs=placed,
        out_specs=(P("dp", "tensor"), P("tensor", None), P(None, "dp")),
        check_vma=False,
    )
```

```python
import functools

import jax
import jax.numpy as jnp
from jax import lax
from jax.experimental import pallas as pl
from jax.experimental.pallas import tpu as pltpu
from jax.sharding import PartitionSpec as P

BLOCK = 128
NX, NY, NZ = 4, 4, 4
STEPS = (0, 1, -1, 2)
ROWS = 128
M_TILE = 256
COST = 40 * 10**9

adapter_scale = 2.0
loss_scale_factor = 64.0


def hi_swap(value):
    return lax.ppermute(value, "tensor", [(t, t ^ 1) for t in range(2 * NX)])


def x_shift(value, step):
    return lax.ppermute(
        value,
        "tensor",
        [(t, ((t // 2 + step) % NX) * 2 + t % 2) for t in range(2 * NX)],
    )


def x_pairs(value, partner):
    return lax.ppermute(
        value, "tensor", [(t, partner[t // 2] * 2 + t % 2) for t in range(2 * NX)]
    )


def core_swap(value):
    return lax.ppermute(value, "dp", [(d, d ^ 1) for d in range(2 * NY * NZ)])


def z_shift(value, step):
    pairs = []
    for d in range(2 * NY * NZ):
        y, z, c = d // (2 * NZ), d // 2 % NZ, d % 2
        pairs.append((d, (y * NZ + (z + step) % NZ) * 2 + c))
    return lax.ppermute(value, "dp", pairs)


def y_shift(value, step):
    n = 2 * NY * NZ
    return lax.ppermute(value, "dp", [(d, (d + step * 2 * NZ) % n) for d in range(n)])


def ring_places(flip, base):
    return [(flip, dx, base) for dx in (0, -1, 1, 2)]


def product_kernel(places, sizes, fresh, *refs):
    count = len(places)
    pieces, projected, down = refs[:count], refs[count], refs[count + 1]
    if fresh:
        blocks = refs[count + 2 : count + 2 + 2 * NY]
        out, ordered, *scratch = refs[count + 2 + 2 * NY :]
    else:
        ordered, _, out, *scratch = refs[count + 2 :]
    w_all, g_all, p_all, o_all, w_sem, g_sem, o_sem, h_sem = scratch
    tensor, group = lax.axis_index("tensor"), lax.axis_index("dp")
    x, hi = tensor // 2, lax.rem(tensor, 2)
    y, z, core = group // (2 * NZ), lax.rem(group // 2, NZ), lax.rem(group, 2)
    tokens, depth = g_all.shape
    k_chunk = depth // NY
    starts = [sum(sizes[:p]) for p in range(count)]

    def token(p):
        flip, dx, start = places[p]
        other = lax.rem(x + dx + NX, NX) * 2 + (1 - hi if flip else hi)
        return pl.multiple_of(other * ROWS + start, sizes[p])

    def piece_copy(p):
        return pltpu.make_async_copy(
            pieces[p], g_all.at[pl.ds(starts[p], sizes[p])], g_sem.at[p]
        )

    def weight_rows(k):
        if not fresh:
            return k * k_chunk
        return pl.multiple_of(lax.rem(y + STEPS[k] + NY, NY) * k_chunk, k_chunk)

    def weight_copies(k):
        if not fresh:
            rows = pl.ds(k * k_chunk, k_chunk)
            yield pltpu.make_async_copy(ordered.at[rows], w_all.at[rows], h_sem.at[k])
            return
        for c in range(2):
            for q in range(NZ):
                zz = lax.rem(z + STEPS[q] + NZ, NZ)
                at = weight_rows(k) + (zz * 2 + (1 - core if c else core)) * BLOCK
                yield pltpu.make_async_copy(
                    blocks[2 * k + c].at[pl.ds(q * BLOCK, BLOCK)],
                    w_all.at[pl.ds(pl.multiple_of(at, BLOCK), BLOCK)],
                    w_sem.at[k, c * NZ + q],
                )

    def out_copy(p):
        return pltpu.make_async_copy(
            o_all.at[pl.ds(starts[p], sizes[p])], out.at[pl.ds(token(p), sizes[p])], o_sem.at[p]
        )

    first = [p for p in range(count) if starts[p] < M_TILE]
    for p in first:
        piece_copy(p).start()
    for k in range(NY):
        for copy in weight_copies(k):
            copy.start()
    for p in range(count):
        if p not in first:
            piece_copy(p).start()
        p_all[starts[p] : starts[p] + sizes[p], :] = projected[pl.ds(token(p), sizes[p]), :]

    for tile in range(tokens // M_TILE):
        low, high = tile * M_TILE, (tile + 1) * M_TILE
        rows = slice(low, high)
        inside = [p for p in range(count) if low <= starts[p] < high]
        for p in inside:
            piece_copy(p).wait()
        total = adapter_scale * jnp.dot(
            p_all[rows, :], down[...], preferred_element_type=jnp.float32
        )
        if tile == 0:
            for k in range(NY):
                for copy in weight_copies(k):
                    copy.wait()
                columns = pl.ds(weight_rows(k), k_chunk)
                total += jnp.dot(
                    g_all[rows, columns], w_all[columns, :], preferred_element_type=jnp.float32
                )
            if fresh:
                pltpu.make_async_copy(w_all, ordered, h_sem.at[0]).start()
        else:
            total += jnp.dot(g_all[rows, :], w_all[...], preferred_element_type=jnp.float32)
        o_all[rows, :] = total.astype(o_all.dtype)
        for p in inside:
            out_copy(p).start()
    for p in range(count):
        out_copy(p).wait()
    if fresh:
        pltpu.make_async_copy(w_all, ordered, h_sem.at[0]).wait()


def product(gathered, projected, down, blocks=None, weights=None, held=None):
    pieces = [piece for values, _ in gathered for piece in values]
    places = [place for _, values in gathered for place in values]
    sizes = [piece.shape[0] for piece in pieces]
    tokens, width = sum(sizes), down.shape[1]
    depth, rank = pieces[0].shape[1], projected.shape[1]
    fresh = blocks is not None
    whole = pl.BlockSpec(memory_space=pltpu.VMEM)
    outside = pl.BlockSpec(memory_space=pl.ANY)
    operands = [*pieces, projected, down]
    specs = [outside] * len(pieces) + [whole, whole]
    result = jax.ShapeDtypeStruct((projected.shape[0], width), jnp.bfloat16)
    scratch = [
        pltpu.VMEM((depth, width), jnp.bfloat16),
        pltpu.VMEM((tokens, depth), jnp.bfloat16),
        pltpu.VMEM((tokens, rank), jnp.bfloat16),
        pltpu.VMEM((tokens, width), jnp.bfloat16),
        pltpu.SemaphoreType.DMA((NY, 2 * NZ)),
        pltpu.SemaphoreType.DMA((len(pieces),)),
        pltpu.SemaphoreType.DMA((len(pieces),)),
        pltpu.SemaphoreType.DMA((NY,)),
    ]
    if fresh:
        operands += blocks
        specs += [outside] * len(blocks)
        outs, out_specs = (result, jax.ShapeDtypeStruct((depth, width), jnp.bfloat16)), (outside, outside)
        aliases = {}
    else:
        aliases = {len(operands) + 1: 0}
        operands += [weights, held]
        specs += [outside, outside]
        outs, out_specs = result, outside
    return pl.pallas_call(
        functools.partial(product_kernel, places, sizes, fresh),
        out_shape=outs,
        in_specs=specs,
        out_specs=out_specs,
        input_output_aliases=aliases,
        scratch_shapes=scratch,
        compiler_params=pltpu.CompilerParams(vmem_limit_bytes=56 * 1024 * 1024),
        cost_estimate=pl.CostEstimate(
            flops=4 * tokens * width * depth,
            bytes_accessed=2 * (tokens + width) * depth + 2 * tokens * width,
            transcendentals=0,
        ),
    )(*operands)


def last_kernel(places, *refs):
    count = len(places)
    pieces = refs[:count]
    projected, down, weights, _, out, o_all, o_sem = refs[count:]
    tensor = lax.axis_index("tensor")
    x, hi = tensor // 2, lax.rem(tensor, 2)
    size = pieces[0].shape[0]

    def token(p):
        flip, dx, start = places[p]
        other = lax.rem(x + dx + NX, NX) * 2 + (1 - hi if flip else hi)
        return pl.multiple_of(other * ROWS + start, size)

    rows = jnp.concatenate([piece[...] for piece in pieces], axis=0)
    narrow = jnp.concatenate([projected[pl.ds(token(p), size), :] for p in range(count)], axis=0)
    total = adapter_scale * jnp.dot(narrow, down[...], preferred_element_type=jnp.float32)
    total += jnp.dot(rows, weights[...], preferred_element_type=jnp.float32)
    o_all[...] = total.astype(o_all.dtype)
    copies = [
        pltpu.make_async_copy(
            o_all.at[pl.ds(p * size, size)], out.at[pl.ds(token(p), size)], o_sem.at[p]
        )
        for p in range(count)
    ]
    for copy in copies:
        copy.start()
    for copy in copies:
        copy.wait()


def last_product(gathered, projected, down, weights, held):
    (pieces, places), = gathered
    tokens, width = pieces[0].shape[0] * len(pieces), down.shape[1]
    depth = pieces[0].shape[1]
    whole = pl.BlockSpec(memory_space=pltpu.VMEM)
    outside = pl.BlockSpec(memory_space=pl.ANY)
    operands = [*pieces, projected, down, weights, held]
    return pl.pallas_call(
        functools.partial(last_kernel, places),
        out_shape=jax.ShapeDtypeStruct(held.shape, held.dtype),
        in_specs=[whole] * (len(operands) - 1) + [outside],
        out_specs=outside,
        input_output_aliases={len(operands) - 1: 0},
        scratch_shapes=[
            pltpu.VMEM((tokens, width), held.dtype),
            pltpu.SemaphoreType.DMA((len(pieces),)),
        ],
        compiler_params=pltpu.CompilerParams(vmem_limit_bytes=24 * 1024 * 1024),
        cost_estimate=pl.CostEstimate(
            flops=2 * tokens * width * depth,
            bytes_accessed=2 * (tokens + width) * depth + 2 * tokens * width,
            transcendentals=0,
        ),
    )(*operands)


def local(kernel, outs, flops, *operands):
    return pl.pallas_call(
        kernel,
        out_shape=outs,
        in_specs=[pl.BlockSpec(memory_space=pltpu.VMEM)] * len(operands),
        out_specs=jax.tree.map(lambda _: pl.BlockSpec(memory_space=pltpu.VMEM), outs),
        compiler_params=pltpu.CompilerParams(vmem_limit_bytes=24 * 1024 * 1024),
        cost_estimate=pl.CostEstimate(flops=flops, bytes_accessed=8 * 2**20, transcendentals=0),
    )(*operands)


def dot(left, right, left_dim, right_dim):
    return lax.dot_general(
        left, right, (((left_dim,), (right_dim,)), ((), ())), preferred_element_type=jnp.float32
    )


def first_kernel(attention, down_t, gradient, up, parcel):
    rank = down_t.shape[0]
    half = ROWS // 2
    projected = dot(gradient[...], up[...], 1, 1).astype(parcel.dtype)
    partial = dot(attention[...], down_t[...], 1, 1)
    high = partial.astype(parcel.dtype)
    low = (partial - high.astype(jnp.float32)).astype(parcel.dtype)
    for t in range(parcel.shape[0]):
        parcel[t, :ROWS, :rank] = high[t * ROWS : (t + 1) * ROWS]
        parcel[t, :ROWS, rank:] = low[t * ROWS : (t + 1) * ROWS]
        parcel[t, ROWS:, :rank] = projected[:half]
        parcel[t, ROWS:, rank:] = projected[half:]


def second_kernel(arrived, attention, gradient, parcel, projected):
    rank = projected.shape[1]
    sources = arrived.shape[0]
    half = ROWS // 2
    sums = arrived[0, :ROWS].astype(jnp.float32)
    for t in range(1, sources):
        sums += arrived[t, :ROWS].astype(jnp.float32)
    adapted = sums[:, :rank] + sums[:, rank:]
    for t in range(sources):
        projected[t * ROWS : t * ROWS + half, :] = arrived[t, ROWS:, :rank]
        projected[t * ROWS + half : (t + 1) * ROWS, :] = arrived[t, ROWS:, rank:]
    up_term = dot(adapted.astype(gradient.dtype), gradient[...], 0, 0).astype(parcel.dtype)
    down_term = dot(projected[...], attention[...], 0, 0).astype(parcel.dtype)
    across = down_term.shape[1] // 128
    for d in range(parcel.shape[0]):
        parcel[d, :rank, :] = up_term[:, d * 128 : (d + 1) * 128]
        a, b = d // across, d % across
        parcel[d, rank:, :] = down_term[a * 16 : (a + 1) * 16, b * 128 : (b + 1) * 128]


def third_kernel(factor, arrived, up_parcel, down_parcel):
    rank = up_parcel.shape[0]
    total = arrived[0].astype(jnp.float32)
    for d in range(1, arrived.shape[0]):
        total += arrived[d].astype(jnp.float32)
    total *= factor
    up_parcel[...] = total[:rank]
    for d in range(down_parcel.shape[0]):
        down_parcel[d] = total[rank:]


def body(
    attention_output,
    output_gradient,
    codes,
    block_scale_values,
    adapter_down_factor,
    adapter_up_factor,
):
    f32, bf16 = jnp.float32, jnp.bfloat16
    n_dp, n_tensor = lax.axis_size("dp"), lax.axis_size("tensor")
    rank = adapter_down_factor.shape[1]
    down_t = adapter_down_factor.T
    half = ROWS // 2
    stage = lax.optimization_barrier

    scaled = (codes.astype(f32) * jnp.repeat(block_scale_values, BLOCK, axis=0)).astype(bf16).T
    own_before, own_behind = x_shift(output_gradient, 1), x_shift(output_gradient, -1)
    z_blocks = [scaled] + [z_shift(scaled, -step) for step in STEPS[1:]]
    parcel = local(
        first_kernel,
        jax.ShapeDtypeStruct((n_tensor, ROWS + ROWS // 2, 2 * rank), bf16),
        COST,
        attention_output, down_t, output_gradient, adapter_up_factor,
    )
    parcel = lax.all_to_all(parcel, "tensor", 0, 0, tiled=True)
    mine = jnp.concatenate(z_blocks, axis=0)
    top, bottom, whole = output_gradient[:half], output_gradient[half:], output_gradient

    mine, top, bottom, whole, own_before, own_behind = stage(
        (mine, top, bottom, whole, own_before, own_behind)
    )
    first = hi_swap(top)
    own_far = x_shift(whole, 2)
    y_blocks = [mine] + [y_shift(mine, -step) for step in STEPS[1:3]]
    mine_swapped = core_swap(mine)
    parcel, projected = local(
        second_kernel,
        (
            jax.ShapeDtypeStruct((n_dp, rank + 16, 128), bf16),
            jax.ShapeDtypeStruct((n_tensor * ROWS, rank), bf16),
        ),
        COST,
        parcel, attention_output, output_gradient,
    )
    parcel = lax.all_to_all(parcel, "dp", 0, 0, tiled=True)

    first, own_far, mine, mine_swapped, bottom, projected, *y_blocks = stage(
        (first, own_far, mine, mine_swapped, bottom, projected, *y_blocks)
    )
    second = hi_swap(bottom)
    first_ring = [first, x_shift(first, 1), x_shift(first, -1), x_shift(first, 2)]
    y_blocks.append(y_shift(mine, -STEPS[3]))
    up_parcel, down_parcel = local(
        functools.partial(third_kernel, adapter_scale / loss_scale_factor),
        (
            jax.ShapeDtypeStruct((rank, 128), f32),
            jax.ShapeDtypeStruct((n_dp, 16, 128), f32),
        ),
        COST,
        parcel,
    )

    second, *rest = stage((second, *first_ring, *y_blocks))
    first_ring, y_blocks = rest[:4], rest[4:]
    blocks = [y_blocks[0], mine_swapped]
    for block in y_blocks[1:]:
        blocks += [block, core_swap(block)]
    second_ring = [second, x_shift(second, 1), x_shift(second, -1), x_shift(second, 2)]
    own_ring = [output_gradient, own_before, own_behind, own_far]
    input_gradient, weights = product(
        [(own_ring, ring_places(0, 0)), (first_ring, ring_places(1, 0))],
        projected, down_t, blocks=blocks,
    )
    up_parcel, down_parcel, input_gradient = stage((up_parcel, down_parcel, input_gradient))
    down_parcel = lax.all_to_all(down_parcel, "dp", 0, 0, tiled=True)
    up_part = up_parcel + x_pairs(up_parcel, (1, 0, 3, 2))
    up_part = up_part + x_pairs(up_part, (3, 2, 1, 0))

    up_part, input_gradient, *second_ring = stage((up_part, input_gradient, *second_ring))
    up_factor_gradient = up_part + hi_swap(up_part)
    down_factor_gradient = (
        down_parcel.reshape(rank // 16, -1, 16, 128).transpose(0, 2, 1, 3).reshape(rank, -1).T
    )
    input_gradient = last_product(
        [(second_ring, ring_places(1, half))],
        projected, down_t, weights=weights, held=input_gradient,
    )
    return (input_gradient, down_factor_gradient, up_factor_gradient)


def solution(mesh):
    placed = (
        P("dp", "tensor"),
        P(("dp", "tensor"), None),
        P("tensor", "dp"),
        P("tensor", "dp"),
        P("tensor", None),
        P(),
    )
    return jax.shard_map(
        body,
        mesh=mesh,
        in_specs=placed,
        out_specs=(P("dp", "tensor"), P("tensor", None), P(None, "dp")),
        check_vma=False,
    )
```
